32 devices in a mesh: pool: 8 (over z, x), tp: 4 (over y, core).
Axes of the slice: x: 2, y: 2, z: 4, core: 2. Of those that a mesh axis runs over, the one named last changes fastest.
Arguments:
- activations: bfloat16 [2, 256, 8192], P(None, None, 'tp'), may hold values from -6 to 6
- gate_matrix: bfloat16 [8192, 28672], P('tp', 'pool'), may hold values from -0.0625 to 0.0625
- up_weight: bfloat16 [8192, 28672], P('tp', 'pool'), may hold values from -0.0625 to 0.0625
- down_matrix: bfloat16 [28672, 8192], P('pool', 'tp'), may hold values from -0.03125 to 0.03125
- shrink_pages: bfloat16 [32, 64, 8192], P('pool', None, 'tp'), may hold values from -0.0625 to 0.0625
- expand_pages: bfloat16 [32, 64, 28672], P('pool', 'tp'), may hold values from -0.75 to 0.75
- row_adapter: int32 [2, 256], replicated, may hold values from 0 to 31, as said below
- page_table: int32 [32], replicated, may hold values from 0 to 31, as said below
Outputs:
- layer_out: bfloat16 [2, 256, 8192], P(None, None, 'tp')
The draws below stay inside these ranges and needn't reach their ends.
Inputs may be any that keep to these rules, and one draw needn't show every extreme that they name: `row_adapter`: in each micro-batch, the rows use at most 1 distinct adapter among those whose pages have the same owner, the owner of page g being g // 4 (so a micro-batch may use up to 8 adapters, one per owner). A permutation: adapter a is stored at page page_table[a].
All inputs are finite; a program needn't handle non-finite values.
Results may differ from the reference program's by a relative error of at most 0.0057.
Values may be sent and summed in bfloat16 or wider, within the bound.
No kernel may reach another device: no remote copies, remote signals or barrier semaphores. Data moves between devices by JAX's collectives and lax.ppermute only.
A program may use at most 128 MiB of HBM per device.

```python
import math
import jax
import jax.numpy as jnp
from jax import lax

MODEL_WIDTH = 8192
FF = 28672
R = 64
ROWS = 256
MB = 2
PAGES = 4
CAP = 1
ADAPTERS = 32


def adapter_tables(key):
    base_key = jax.random.fold_in(key, 11)
    page_table = jax.random.permutation(jax.random.fold_in(base_key, 1), ADAPTERS).astype(jnp.int32)
    adapter_at = jnp.argsort(page_table, stable=True).astype(jnp.int32)
    owners = ADAPTERS // PAGES
    batch_ids = jnp.arange(MB, dtype=jnp.int32)
    first_page = page_table[0]
    last_page = page_table[ADAPTERS - 1]
    target_page = jnp.where(batch_ids == 0, last_page, first_page).astype(jnp.int32)
    target_owner = (target_page // PAGES).astype(jnp.int32)
    starts = jax.random.randint(jax.random.fold_in(base_key, 2), (MB, owners), 0, PAGES).astype(jnp.int32)
    owner_ids = jnp.arange(owners, dtype=jnp.int32)
    starts = jnp.where(owner_ids[None, :] == target_owner[:, None], (target_page % PAGES)[:, None], starts)
    offsets = (starts[:, :, None] + jnp.arange(CAP, dtype=jnp.int32)) % PAGES
    candidates = (owner_ids[None, :, None] * PAGES + offsets).reshape(MB, owners * CAP).astype(jnp.int32)
    live_owner = jax.random.randint(jax.random.fold_in(base_key, 3), (MB, owners), 0, 2) == 1
    live_owner = live_owner | (owner_ids[None, :] == target_owner[:, None])
    live_flat = jnp.repeat(live_owner, CAP, axis=1)
    cand_count = owners * CAP
    levels = jnp.power(2, jax.random.randint(jax.random.fold_in(base_key, 5), (MB, cand_count), 0, 4)).astype(jnp.int32)
    noise = jax.random.randint(jax.random.fold_in(base_key, 6), (MB, ROWS, cand_count), 0, 65536)
    scores = noise * levels[:, None, :] * cand_count + jnp.arange(cand_count, dtype=jnp.int32)
    scores = jnp.where(live_flat[:, None, :], scores, -1).astype(jnp.int32)
    picked = lax.top_k(scores, 1)[1]
    spread = jnp.broadcast_to(candidates[:, None, :], (MB, ROWS, cand_count))
    page_pick = jnp.take_along_axis(spread, picked, axis=2)[:, :, 0]
    page_pick = page_pick.at[0, 0].set(last_page)
    if MB > 1:
        page_pick = page_pick.at[MB - 1, 0].set(first_page)
    else:
        page_pick = page_pick.at[0, 1].set(first_page)
    row_adapter = jnp.take(adapter_at, page_pick.astype(jnp.int32), axis=0).astype(jnp.int32)
    return (page_table, row_adapter)


def draw_page_table(key, part):
    return adapter_tables(key)[0]


def draw_row_adapter(key, part):
    return adapter_tables(key)[1]


def shard_levels(key, dims, cuts, smallest, top_value):
    factor_of, own = 1.0, jax.random.fold_in(key, 6)
    for position, parts in cuts:
        heights = jnp.exp(jax.random.uniform(jax.random.fold_in(own, position), (parts,), jnp.float32, smallest / len(cuts), top_value / len(cuts)))
        factor_of = factor_of * jnp.repeat(heights, dims[position] // parts).reshape([-1 if axis == position else 1 for axis in range(len(dims))])
    return factor_of


def centred(own_key, shape, width, most, cuts=(), kind=jnp.bfloat16):
    values = width * jax.random.normal(own_key, shape, jnp.float32)
    if cuts:
        values = values * shard_levels(own_key, shape, cuts, -0.22, 0.18)
    return jnp.clip(values, -most, most).astype(kind)


def setup_inputs(seed: int = 0) -> dict:
    seeds = jax.random.split(jax.random.key(seed), 9)
    activations = centred(seeds[0], (MB, ROWS, MODEL_WIDTH), 1.0, 6.0, ((2, 4),))
    gate_matrix = centred(seeds[1], (MODEL_WIDTH, FF), MODEL_WIDTH ** -0.5, 0.0625, ((0, 4), (1, 8)))
    up_weight = centred(seeds[2], (MODEL_WIDTH, FF), MODEL_WIDTH ** -0.5, 0.0625, ((0, 4), (1, 8)))
    down_matrix = centred(seeds[3], (FF, MODEL_WIDTH), FF ** -0.5, 0.03125, ((0, 8), (1, 4)))
    shrink_pages = centred(seeds[4], (ADAPTERS, R, MODEL_WIDTH), MODEL_WIDTH ** -0.5, 0.0625, ((0, 8), (2, 4)))
    expand_pages = centred(seeds[5], (ADAPTERS, R, FF), R ** -0.5, 0.75, ((0, 8), (1, 4)))
    row_adapter = draw_row_adapter(jax.random.fold_in(seeds[8], 71), 0)
    page_table = draw_page_table(jax.random.fold_in(seeds[8], 71), 0)
    return dict(activations=activations, gate_matrix=gate_matrix, up_weight=up_weight, down_matrix=down_matrix, shrink_pages=shrink_pages, expand_pages=expand_pages, row_adapter=row_adapter, page_table=page_table)


adapter_scale = 2.0


def reference(activations, gate_matrix, up_weight, down_matrix, shrink_pages, expand_pages, row_adapter, page_table):
    catalog = jnp.arange(ADAPTERS, dtype=jnp.int32)
    page_of_row = jnp.sum(jnp.where(row_adapter[:, :, None] == catalog, page_table, 0), axis=2).astype(jnp.int32)
    row_total = MB * ROWS
    flattened_rows = activations.reshape(row_total, MODEL_WIDTH)
    row_pages = page_of_row.reshape(row_total)
    rows_per_block = math.gcd(row_total, 32)

    def adapter_block(packed_weights):
        rows_blk, pages_blk = packed_weights
        shrink_rows = jnp.take(shrink_pages, pages_blk, axis=0)
        low_rank = jnp.einsum("nd,nkd->nk", rows_blk.astype(jnp.float32), shrink_rows.astype(jnp.float32),
                              precision=lax.Precision.HIGHEST).astype(jnp.bfloat16)
        expand_rows = jnp.take(expand_pages, pages_blk, axis=0)
        return jnp.einsum("nk,nkf->nf", low_rank.astype(jnp.float32), expand_rows.astype(jnp.float32),
                          precision=lax.Precision.HIGHEST)

    adapter_delta = lax.map(adapter_block, (flattened_rows.reshape(-1, rows_per_block, MODEL_WIDTH),
                                  row_pages.reshape(-1, rows_per_block))).reshape(row_total, FF)
    gate_value = jnp.dot(flattened_rows, gate_matrix, preferred_element_type=jnp.float32)
    up_activation = jnp.dot(flattened_rows, up_weight, preferred_element_type=jnp.float32) + adapter_scale * adapter_delta
    hidden = (jax.nn.silu(gate_value) * up_activation).astype(jnp.bfloat16)
    layer_out = jnp.dot(hidden, down_matrix, preferred_element_type=jnp.float32).astype(jnp.bfloat16)
    return layer_out.reshape(MB, ROWS, MODEL_WIDTH)
```

```python
import functools

import jax
import jax.numpy as jnp
from jax import lax
from jax.experimental import pallas as pl
from jax.experimental.pallas import tpu as pltpu
from jax.sharding import PartitionSpec as P

ADAPTER_SCALE = 2.0
VMEM_LIMIT = 48 * 1024 * 1024
BF16 = jnp.bfloat16
F32 = jnp.float32


def tile_of(size, choices):
    return next((c for c in choices if size % c == 0), size)


def exchange(x, axis, bit):
    return lax.ppermute(x, axis, [(i, i ^ bit) for i in range(lax.axis_size(axis))])


def params():
    return pltpu.CompilerParams(vmem_limit_bytes=VMEM_LIMIT)


def pick_pages(expand_pages, chosen, pool_count):
    _, ranks, hidden = expand_pages.shape
    width = hidden // pool_count

    def body(chosen_ref, page_ref, out_ref):
        out_ref[...] = page_ref[...]

    return pl.pallas_call(
        body,
        grid_spec=pltpu.PrefetchScalarGridSpec(
            num_scalar_prefetch=1,
            grid=(pool_count,),
            in_specs=[pl.BlockSpec((None, ranks, width), lambda i, c: (c[0], 0, i))],
            out_specs=pl.BlockSpec((None, ranks, width), lambda i, c: (i, 0, 0)),
        ),
        out_shape=jax.ShapeDtypeStruct((pool_count, ranks, width), BF16),
        compiler_params=params(),
        name="pick_pages",
    )(chosen, expand_pages)


def project(tp_index, activations, batch, start, rows, weight, wide=None, factors=None):
    tp = lax.axis_size("tp")
    block = rows // tp
    depth, hidden = weight.shape
    tile = tile_of(hidden, (512, 256, 128))
    order = [*range(0, tp, 2), *range(1, tp, 2)]
    half = tp // 2

    def body(t_ref, *refs):
        x_refs, refs = refs[:tp], refs[tp:]
        w_ref, refs = refs[0], refs[1:]
        if wide is not None:
            wide_refs, e_ref, refs = refs[:tp], refs[tp], refs[tp + 1 :]
        keep_ref, send_ref, xs = refs[:3]

        @pl.when(pl.program_id(0) == 0)
        def _():
            for k, x_ref in enumerate(x_refs):
                xs[k * block : (k + 1) * block, :] = x_ref[...]
            if wide is not None:
                for k, r_ref in enumerate(wide_refs):
                    refs[3][k * block : (k + 1) * block, :] = r_ref[...]

        acc = jnp.dot(xs[...], w_ref[...], preferred_element_type=F32)
        if wide is not None:
            acc += jnp.dot(refs[3][...], e_ref[...], preferred_element_type=F32)
        acc = acc.reshape(2, half, block, tile)
        keep_ref[...] = acc[0]
        send_ref[...] = acc[1].astype(BF16)

    first = start // block

    def x_spec(r, width):
        return pl.BlockSpec((None, block, width), lambda i, t: (batch, first + (t[0] ^ r), 0))

    in_specs = [x_spec(r, depth) for r in order] + [pl.BlockSpec((depth, tile), lambda i, t: (0, i))]
    operands = [activations] * tp + [weight]
    scratch = [pltpu.VMEM((rows, depth), BF16)]
    if wide is not None:
        slots = factors.shape[0]
        in_specs += [x_spec(r, slots) for r in order]
        in_specs += [pl.BlockSpec((slots, tile), lambda i, t: (0, i))]
        operands += [wide] * tp + [factors]
        scratch += [pltpu.VMEM((rows, slots), BF16)]
    out_spec = pl.BlockSpec((half, block, tile), lambda i, t: (0, 0, i))
    return pl.pallas_call(
        body,
        grid_spec=pltpu.PrefetchScalarGridSpec(
            num_scalar_prefetch=1,
            grid=(hidden // tile,),
            in_specs=in_specs,
            out_specs=[out_spec, out_spec],
            scratch_shapes=scratch,
        ),
        out_shape=[
            jax.ShapeDtypeStruct((half, block, hidden), F32),
            jax.ShapeDtypeStruct((half, block, hidden), BF16),
        ],
        compiler_params=params(),
        cost_estimate=pl.CostEstimate(
            flops=2 * rows * depth * hidden, bytes_accessed=2 * depth * hidden, transcendentals=0
        ),
        name="gate" if wide is None else "up",
    )(tp_index, *operands)


def scatter_sum(keep, send):
    bit = 1
    while True:
        got = exchange(send, "tp", bit)
        if keep.shape[0] == 1:
            return [keep[0], got[0]]
        total = keep[1::2] + got[1::2].astype(F32)
        keep = keep[0::2] + got[0::2].astype(F32)
        send = total.astype(BF16)
        bit *= 2


def gather_rows(block):
    tp = lax.axis_size("tp")
    blocks = [block]
    bit = tp // 2
    found = {0: block}
    while bit:
        for r in list(found):
            found[r ^ bit] = exchange(found[r], "tp", bit)
        bit //= 2
    return [found[r] for r in range(tp)]


def down_project(pool_index, blocks, weight, width):
    pool = lax.axis_size("pool")
    tp = len(blocks)
    block, depth = blocks[0].shape
    rows = tp * block
    half = pool // 2

    def body(p_ref, *refs):
        h_refs, w_ref, keep_ref, send_ref, hs = refs[:tp], *refs[tp:]
        step = pl.program_id(0)

        @pl.when(step == 0)
        def _():
            for k, h_ref in enumerate(h_refs):
                hs[k * block : (k + 1) * block, :] = h_ref[...]

        acc = jnp.dot(hs[...], w_ref[...], preferred_element_type=F32)

        @pl.when(step < half)
        def _():
            send_ref[...] = acc.astype(BF16)

        @pl.when(step >= half)
        def _():
            keep_ref[...] = acc

    def column(i, p):
        q = jnp.where(i < half, 2 * i + 1, 2 * (i - half))
        return (0, p[0] ^ q)

    return pl.pallas_call(
        body,
        grid_spec=pltpu.PrefetchScalarGridSpec(
            num_scalar_prefetch=1,
            grid=(pool,),
            in_specs=[pl.BlockSpec((block, depth), lambda i, p: (0, 0))] * tp
            + [pl.BlockSpec((depth, width), column)],
            out_specs=[
                pl.BlockSpec((None, rows, width), lambda i, p: (jnp.maximum(i - half, 0), 0, 0)),
                pl.BlockSpec((None, rows, width), lambda i, p: (jnp.minimum(i, half - 1), 0, 0)),
            ],
            scratch_shapes=[pltpu.VMEM((rows, depth), BF16)],
        ),
        out_shape=[
            jax.ShapeDtypeStruct((half, rows, width), F32),
            jax.ShapeDtypeStruct((half, rows, width), BF16),
        ],
        compiler_params=params(),
        cost_estimate=pl.CostEstimate(
            flops=2 * rows * depth * width * pool,
            bytes_accessed=2 * depth * width * pool,
            transcendentals=0,
        ),
        name="down",
    )(pool_index, *blocks, weight)


def pool_sum(keep, send):
    pool = lax.axis_size("pool")
    bit = 1
    while True:
        got = exchange(send, "pool", bit)
        if keep.shape[0] == 1:
            break
        send = (keep[1::2] + got[1::2].astype(F32)).astype(BF16)
        keep = keep[0::2] + got[0::2].astype(F32)
        bit *= 2
    held = (keep + got.astype(F32)).astype(BF16)
    parts = [(held, [0])]
    while bit:
        have = jnp.concatenate([a for a, _ in parts]) if len(parts) > 1 else parts[0][0]
        index = [q for _, qs in parts for q in qs]
        parts.append((exchange(have, "pool", bit), [q ^ bit for q in index]))
        bit //= 2
    return parts


def assemble(tp_index, pool_index, parts, tp):
    pool = lax.axis_size("pool")
    _, rows, width = parts[0][0].shape
    block = rows // tp
    order = [(k, j, q) for k, (_, qs) in enumerate(parts) for j, q in enumerate(qs)]
    begins = [next(s for s, o in enumerate(order) if o[0] == k) for k in range(len(parts))]

    def body(t_ref, p_ref, *refs):
        out_ref = refs[-1]
        step = pl.program_id(0)
        for k, (_, qs) in enumerate(parts):

            @pl.when((step >= begins[k]) & (step < begins[k] + len(qs)))
            def _(k=k):
                for r in range(tp):
                    at = pl.multiple_of((t_ref[0] ^ r) * block, block)
                    out_ref[pl.ds(at, block), :] = refs[k][r * block : (r + 1) * block, :]

    def out_column(i, t, p):
        q = sum(jnp.where(i == s, o[2], 0) for s, o in enumerate(order))
        return (0, p[0] ^ q)

    def in_block(begin, count):
        return lambda i, t, p: (jnp.clip(i - begin, 0, count - 1), 0, 0)

    return pl.pallas_call(
        body,
        grid_spec=pltpu.PrefetchScalarGridSpec(
            num_scalar_prefetch=2,
            grid=(pool,),
            in_specs=[
                pl.BlockSpec((None, rows, width), in_block(begins[k], len(qs)))
                for k, (_, qs) in enumerate(parts)
            ],
            out_specs=pl.BlockSpec((rows, width), out_column),
        ),
        out_shape=jax.ShapeDtypeStruct((rows, width * pool), BF16),
        compiler_params=params(),
        name="assemble",
    )(tp_index, pool_index, *[a for a, _ in parts])


def on_device(
    activations,
    gate_matrix,
    up_weight,
    down_matrix,
    shrink_pages,
    expand_pages,
    row_adapter,
    page_table,
):
    pool = lax.axis_size("pool")
    tp = lax.axis_size("tp")
    pool_index = lax.axis_index("pool")
    tp_index = lax.axis_index("tp")
    p_scalar = pool_index.astype(jnp.int32).reshape(1)
    t_scalar = tp_index.astype(jnp.int32).reshape(1)
    batches, row_count, _ = activations.shape
    page_count, ranks, _ = shrink_pages.shape
    rank_local = expand_pages.shape[1]
    columns = down_matrix.shape[1]

    catalog = jnp.arange(page_table.shape[0], dtype=jnp.int32)
    page_of_row = jnp.sum(jnp.where(row_adapter[:, :, None] == catalog, page_table, 0), axis=2)
    owned = page_of_row // page_count == pool_index
    chosen = jnp.max(jnp.where(owned, page_of_row % page_count, 0), axis=1)

    factors = []
    for m in range(batches):
        outgoing = pick_pages(expand_pages, chosen[m : m + 1], pool)
        received = lax.all_to_all(outgoing, "pool", split_axis=0, concat_axis=0, tiled=True)
        factors.append(received.reshape(pool * rank_local, -1))

    low = []
    for m in range(batches):
        page = lax.dynamic_index_in_dim(shrink_pages, chosen[m], 0, keepdims=False)
        part = lax.dot_general(
            page, activations[m], (((1,), (1,)), ((), ())), preferred_element_type=F32
        )
        low.append(jnp.where(owned[m][None, :], part, 0.0))
    low = jnp.stack(low, axis=1).reshape(tp, rank_local, batches * row_count)
    low = jnp.sum(lax.all_to_all(low, "tp", split_axis=0, concat_axis=0, tiled=True), axis=0)
    low = ADAPTER_SCALE * low.astype(BF16)
    low = lax.all_to_all(
        jnp.broadcast_to(low[None], (pool, *low.shape)), "pool", split_axis=0, concat_axis=0, tiled=True
    )
    wide = low.reshape(pool * rank_local, batches * row_count).T.reshape(
        batches, row_count, pool * rank_local
    )

    chunks = [(m, 0, row_count) for m in range(batches)]
    gates = []
    for m, start, rows in chunks:
        gates.append(scatter_sum(*project(t_scalar, activations, m, start, rows, gate_matrix)))
    outputs = []
    for (m, start, rows), gate in zip(chunks, gates):
        up = scatter_sum(
            *project(t_scalar, activations, m, start, rows, up_weight, wide, factors[m])
        )
        gate_value = gate[0] + gate[1].astype(F32)
        up_value = up[0] + up[1].astype(F32)
        hidden = (jax.nn.silu(gate_value) * up_value).astype(BF16)
        blocks = gather_rows(hidden)
        width = columns // pool
        if width % 128 == 0:
            parts = pool_sum(*down_project(p_scalar, blocks, down_matrix, width))
            outputs.append(assemble(t_scalar, p_scalar, parts, tp))
        else:
            here = jnp.stack(blocks)
            for bit in range(tp.bit_length() - 1):
                pairs = here.reshape(-1, 2, 1 << bit, *here.shape[1:])
                here = jnp.where((tp_index >> bit) & 1, pairs[:, ::-1], pairs).reshape(here.shape)
            partial = jnp.dot(
                here.reshape(rows, -1), down_matrix, preferred_element_type=F32
            )
            outputs.append(lax.psum(partial, "pool").astype(BF16))
    return jnp.concatenate(outputs, axis=0).reshape(batches, row_count, columns)


def solution(mesh):
    in_specs = (
        P(None, None, "tp"),
        P("tp", "pool"),
        P("tp", "pool"),
        P("pool", "tp"),
        P("pool", None, "tp"),
        P("pool", "tp", None),
        P(),
        P(),
    )
    return jax.shard_map(
        on_device, mesh=mesh, in_specs=in_specs, out_specs=P(None, None, "tp"), check_vma=False
    )
```

```python
import jax
import jax.numpy as jnp
from jax import lax
from jax.experimental import pallas as pl
from jax.experimental.pallas import tpu as pltpu
from jax.sharding import PartitionSpec as P

ADAPTER_SCALE = 2.0
VMEM_LIMIT = 48 * 1024 * 1024
BF16 = jnp.bfloat16
F32 = jnp.float32


def tile_of(size, choices):
    return next((c for c in choices if size % c == 0), size)


def exchange(x, axis, bit):
    return lax.ppermute(x, axis, [(i, i ^ bit) for i in range(lax.axis_size(axis))])


def params():
    return pltpu.CompilerParams(vmem_limit_bytes=VMEM_LIMIT)


def pick_pages(pool_index, page_table, row_adapter, expand_pages, page_count, pool_count):
    _, ranks, hidden = expand_pages.shape
    width = hidden // pool_count
    batches, row_count = row_adapter.shape

    def body(p_ref, table_ref, rows_ref, pages_ref, chosen_ref, mask_ref, *refs):
        outs, sems = refs[:batches], refs[batches]
        copies = []
        for m in range(batches):
            rows = rows_ref[m : m + 1, :]
            page = jnp.zeros_like(rows)
            for a in range(page_table.shape[0]):
                page = jnp.where(rows == a, table_ref[a], page)
            local = page - p_ref[0] * page_count
            owned = (local >= 0) & (local < page_count)
            mask_ref[m] = jnp.where(owned, 1.0, 0.0)
            chosen = jnp.max(jnp.where(owned, local, 0))
            chosen_ref[m] = chosen
            for q in range(pool_count):
                source = pages_ref.at[chosen, :, pl.ds(q * width, width)]
                copy = pltpu.make_async_copy(source, outs[m].at[q], sems.at[m * pool_count + q])
                copy.start()
                copies.append(copy)
        for copy in copies:
            copy.wait()

    smem = pl.BlockSpec(memory_space=pltpu.SMEM)
    vmem = pl.BlockSpec(memory_space=pltpu.VMEM)
    hbm = pl.BlockSpec(memory_space=pltpu.HBM)
    chosen, mask, *blocks = pl.pallas_call(
        body,
        in_specs=[smem, smem, vmem, hbm],
        out_specs=[smem, vmem] + [hbm] * batches,
        out_shape=[
            jax.ShapeDtypeStruct((batches,), jnp.int32),
            jax.ShapeDtypeStruct((batches, 1, row_count), F32),
        ]
        + [jax.ShapeDtypeStruct((pool_count, ranks, width), BF16)] * batches,
        scratch_shapes=[pltpu.SemaphoreType.DMA((batches * pool_count,))],
        compiler_params=params(),
        name="pick_pages",
    )(pool_index, page_table, row_adapter, expand_pages)
    return chosen, mask, blocks


def shrink(tp_index, chosen, mask, activations, shrink_pages, tp):
    batches, row_count, depth = activations.shape
    ranks = shrink_pages.shape[1]
    local = ranks // tp

    def body(t_ref, chosen_ref, page_ref, x_ref, mask_ref, keep_ref, send_ref):
        part = lax.dot_general(
            page_ref[...], x_ref[...], (((1,), (1,)), ((), ())), preferred_element_type=F32
        )
        part = jnp.where(mask_ref[...] > 0.5, part, 0.0)
        blocks = [part[k * local : (k + 1) * local] for k in range(tp)]
        for bit in range(tp.bit_length() - 1):
            flip = ((t_ref[0] >> bit) & 1) == 1
            blocks = [jnp.where(flip, blocks[k ^ (1 << bit)], blocks[k]) for k in range(tp)]
        for k in range(tp // 2):
            keep_ref[k] = blocks[2 * k]
            send_ref[k] = blocks[2 * k + 1]

    out_spec = pl.BlockSpec((tp // 2, local, row_count), lambda m, t, c: (0, 0, m))
    return pl.pallas_call(
        body,
        grid_spec=pltpu.PrefetchScalarGridSpec(
            num_scalar_prefetch=2,
            grid=(batches,),
            in_specs=[
                pl.BlockSpec((None, ranks, depth), lambda m, t, c: (c[m], 0, 0)),
                pl.BlockSpec((None, row_count, depth), lambda m, t, c: (m, 0, 0)),
                pl.BlockSpec((None, 1, row_count), lambda m, t, c: (m, 0, 0)),
            ],
            out_specs=[out_spec, out_spec],
        ),
        out_shape=[jax.ShapeDtypeStruct((tp // 2, local, batches * row_count), F32)] * 2,
        compiler_params=params(),
        name="shrink",
    )(tp_index, chosen, shrink_pages, activations, mask)


def project(tp_index, activations, group, start, rows, weight, wide=None, factors=None):
    tp = lax.axis_size("tp")
    block = rows // tp
    depth, hidden = weight.shape
    tile = tile_of(hidden, (896, 512, 256, 128))
    half = tp // 2
    order = [(m, r) for first in (0, 1) for m in group for r in range(first, tp, 2)]
    count = len(order)
    pieces = 0 if wide is None else len(factors)

    def body(t_ref, *refs):
        x_refs, refs = refs[:count], refs[count:]
        w_ref, refs = refs[0], refs[1:]
        if wide is not None:
            wide_refs, e_refs = refs[:count], refs[count : count + pieces]
            refs = refs[count + pieces :]
        keep_ref, send_ref, xs = refs[:3]

        @pl.when(pl.program_id(0) == 0)
        def _():
            for k, x_ref in enumerate(x_refs):
                xs[k * block : (k + 1) * block, :] = x_ref[...]
            if wide is not None:
                for k, r_ref in enumerate(wide_refs):
                    refs[3][k * block : (k + 1) * block, :] = r_ref[...]

        acc = jnp.dot(xs[...], w_ref[...], preferred_element_type=F32)
        if wide is not None:
            e_all = jnp.concatenate([e_ref[...] for e_ref in e_refs], axis=0)
            acc += jnp.dot(refs[3][...], e_all, preferred_element_type=F32)
        acc = acc.reshape(2, len(group), half, block, tile)
        keep_ref[...] = acc[0]
        send_ref[...] = acc[1].astype(BF16)

    first = start // block

    def x_spec(m, r, width):
        return pl.BlockSpec((None, block, width), lambda i, t: (m, first + (t[0] ^ r), 0))

    in_specs = [x_spec(m, r, depth) for m, r in order] + [pl.BlockSpec((depth, tile), lambda i, t: (0, i))]
    operands = [activations] * count + [weight]
    scratch = [pltpu.VMEM((count * block, depth), BF16)]
    if wide is not None:
        slots = wide.shape[-1]
        in_specs += [x_spec(m, r, slots) for m, r in order]
        in_specs += [pl.BlockSpec((slots // pieces, tile), lambda i, t: (0, i))] * pieces
        operands += [wide] * count + list(factors)
        scratch += [pltpu.VMEM((count * block, slots), BF16)]
    out_spec = pl.BlockSpec((len(group), half, block, tile), lambda i, t: (0, 0, 0, i))
    return pl.pallas_call(
        body,
        grid_spec=pltpu.PrefetchScalarGridSpec(
            num_scalar_prefetch=1,
            grid=(hidden // tile,),
            in_specs=in_specs,
            out_specs=[out_spec, out_spec],
            scratch_shapes=scratch,
        ),
        out_shape=[
            jax.ShapeDtypeStruct((len(group), half, block, hidden), F32),
            jax.ShapeDtypeStruct((len(group), half, block, hidden), BF16),
        ],
        compiler_params=params(),
        cost_estimate=pl.CostEstimate(
            flops=2 * count * block * depth * hidden, bytes_accessed=2 * depth * hidden, transcendentals=0
        ),
        name="gate" if wide is None else "up",
    )(tp_index, *operands)


def scatter_sum(keep, send, after=()):
    terms, bit = [keep], 1
    while True:
        last = terms[0].shape[1] == 1
        if last and after:
            send, *after = lax.optimization_barrier((send, *after))
        terms.append(exchange(send, "tp", bit))
        if last:
            terms = [x[:, 0] for x in terms]
            return (terms, after) if after else terms
        send = sum(x[:, 1::2].astype(F32) for x in terms).astype(send.dtype)
        terms = [x[:, 0::2] for x in terms]
        bit *= 2


def gather_rows(block):
    tp = lax.axis_size("tp")
    blocks = [block]
    bit = tp // 2
    found = {0: block}
    while bit:
        for r in list(found):
            found[r ^ bit] = exchange(found[r], "tp", bit)
        bit //= 2
    return [found[r] for r in range(tp)]


def down_project(pool_index, blocks, weight, first, columns):
    pool = lax.axis_size("pool")
    tp = len(blocks)
    block, depth = blocks[0].shape
    rows = tp * block
    half = pool // 2
    piece = rows // pool
    per_block = block // piece
    tile = tile_of(columns, (512, 256, 128))

    def body(p_ref, *refs):
        h_refs, w_ref, keep_ref, send_ref, hs = refs[:tp], *refs[tp:]

        @pl.when(pl.program_id(0) == 0)
        def _():
            for k in range(pool):
                q = p_ref[0] ^ k
                at = pl.multiple_of(((q & 1) * half + (q >> 1)) * piece, piece)
                j = k % per_block
                hs[pl.ds(at, piece), :] = h_refs[k // per_block][j * piece : (j + 1) * piece, :]

        acc = jnp.dot(hs[...], w_ref[...], preferred_element_type=F32)
        acc = acc.reshape(2, half, piece, tile)
        keep_ref[...] = acc[0]
        send_ref[...] = acc[1].astype(BF16)

    out_spec = pl.BlockSpec((half, piece, tile), lambda i, p: (0, 0, i))
    return pl.pallas_call(
        body,
        grid_spec=pltpu.PrefetchScalarGridSpec(
            num_scalar_prefetch=1,
            grid=(columns // tile,),
            in_specs=[pl.BlockSpec((block, depth), lambda i, p: (0, 0))] * tp
            + [pl.BlockSpec((depth, tile), lambda i, p: (0, first // tile + i))],
            out_specs=[out_spec, out_spec],
            scratch_shapes=[pltpu.VMEM((rows, depth), BF16)],
        ),
        out_shape=[
            jax.ShapeDtypeStruct((half, piece, columns), F32),
            jax.ShapeDtypeStruct((half, piece, columns), BF16),
        ],
        compiler_params=params(),
        cost_estimate=pl.CostEstimate(
            flops=2 * rows * depth * columns, bytes_accessed=2 * depth * columns, transcendentals=0
        ),
        name="down",
    )(pool_index, *blocks, weight)


def pool_sum(keep, send):
    terms, bit = [keep], 1
    while True:
        terms.append(exchange(send, "pool", bit))
        if terms[0].shape[0] == 1:
            break
        send = sum(x[1::2].astype(F32) for x in terms).astype(BF16)
        terms = [x[0::2] for x in terms]
        bit *= 2
    parts = [(sum(x.astype(F32) for x in terms).astype(BF16), [0])]
    while bit:
        have = jnp.concatenate([x for x, _ in parts]) if len(parts) > 1 else parts[0][0]
        order = [q ^ bit for _, qs in parts for q in qs]
        parts.append((exchange(have, "pool", bit), order))
        bit //= 2
    return parts


def place(tp_index, pool_index, parts, out, shape, batch, start, first):
    pool = sum(len(qs) for _, qs in parts)
    tp = lax.axis_size("tp")
    _, piece, columns = parts[0][0].shape
    per_block = pool // tp

    def body(t_ref, p_ref, *refs):
        out_ref, sems = refs[-2:]
        copies = []
        for part_ref, (_, qs) in zip(refs, parts):
            for j, q in enumerate(qs):
                k = p_ref[0] ^ q
                block = t_ref[0] ^ (k // per_block)
                at = pl.multiple_of(start + (block * per_block + k % per_block) * piece, piece)
                target = out_ref.at[batch, pl.ds(at, piece), pl.ds(first, columns)]
                copies.append(pltpu.make_async_copy(part_ref.at[j], target, sems.at[q]))
        for copy in copies:
            copy.start()
        for copy in copies:
            copy.wait()

    held = [] if out is None else [out]
    return pl.pallas_call(
        body,
        in_specs=[pl.BlockSpec(memory_space=pltpu.SMEM)] * 2
        + [pl.BlockSpec(memory_space=pl.ANY)] * (len(parts) + len(held)),
        out_specs=pl.BlockSpec(memory_space=pl.ANY),
        out_shape=jax.ShapeDtypeStruct(shape, BF16),
        scratch_shapes=[pltpu.SemaphoreType.DMA((pool,))],
        input_output_aliases={2 + len(parts): 0} if held else {},
        compiler_params=params(),
        name="place",
    )(tp_index, pool_index, *[x for x, _ in parts], *held)


def by_index(x, index):
    for bit in range(x.shape[0].bit_length() - 1):
        pairs = x.reshape(-1, 2, 1 << bit, *x.shape[1:])
        x = jnp.where((index >> bit) & 1, pairs[:, ::-1], pairs).reshape(x.shape)
    return x


def on_device(
    activations,
    gate_matrix,
    up_weight,
    down_matrix,
    shrink_pages,
    expand_pages,
    row_adapter,
    page_table,
):
    pool = lax.axis_size("pool")
    tp = lax.axis_size("tp")
    pool_index = lax.axis_index("pool")
    tp_index = lax.axis_index("tp")
    p_scalar = pool_index.astype(jnp.int32).reshape(1)
    t_scalar = tp_index.astype(jnp.int32).reshape(1)
    batches, row_count, _ = activations.shape
    page_count = shrink_pages.shape[0]
    rank_local = expand_pages.shape[1]
    columns = down_matrix.shape[1]
    chunks = [(m, 0, row_count) for m in range(batches)]

    def across(x):
        return lax.all_to_all(x, "pool", split_axis=0, concat_axis=0, tiled=True)

    chosen, mask, picked = pick_pages(
        p_scalar, page_table, row_adapter, expand_pages, page_count, pool
    )
    factors = [across(picked[0])]
    low = shrink(t_scalar, chosen, mask, activations, shrink_pages, tp)
    low = sum(scatter_sum(*(x[None] for x in low)))
    low = ADAPTER_SCALE * low.astype(BF16)
    ready, rows_in = lax.optimization_barrier((low, activations))
    gate = project(t_scalar, rows_in, range(batches), 0, row_count, gate_matrix)
    wide, bit = ready, 1
    while 4 * bit < pool:
        wide = jnp.concatenate([wide, exchange(wide, "pool", bit)])
        bit *= 2
    gate, (wide, *outgoing) = scatter_sum(*gate, (wide, *picked[1:]))
    while bit < pool:
        wide = jnp.concatenate([wide, exchange(wide, "pool", bit)])
        bit *= 2
    wide = wide.reshape(pool, rank_local, -1)
    factors += [across(x) for x in outgoing]
    wide = by_index(wide, pool_index)
    wide = wide.reshape(pool * rank_local, batches * row_count).T
    wide = wide.reshape(batches, row_count, pool * rank_local)
    factors = [x.reshape(pool * rank_local, -1) for x in factors]
    apart = row_count % (16 * pool) == 0 and pool % tp == 0 and columns % 512 == 0
    out = None
    outputs = []
    rows_in = activations
    for m, start, rows in chunks:
        up = project(t_scalar, rows_in, (m,), start, rows, up_weight, wide, [factors[m]])
        held = 0 if apart else len(gate) - 1
        up, gate[held:] = scatter_sum(*up, gate[held:])
        gate_value = sum(x[m].astype(F32) for x in gate)
        up_value = sum(x[0].astype(F32) for x in up)
        hidden = (jax.nn.silu(gate_value) * up_value).astype(BF16)
        hidden, rows_in = lax.optimization_barrier((hidden, rows_in))
        blocks = gather_rows(hidden)
        if apart:
            groups = 2
            width = columns // groups
            for g in range(groups):
                pieces = pool_sum(
                    *down_project(p_scalar, blocks, down_matrix, g * width, width)
                )
                out = place(
                    t_scalar, p_scalar, pieces, out, (batches, row_count, columns), m, start, g * width
                )
        else:
            here = by_index(jnp.stack(blocks), tp_index).reshape(rows, -1)
            partial = jnp.dot(here, down_matrix, preferred_element_type=F32)
            outputs.append(lax.psum(partial, "pool").astype(BF16))
    if out is not None:
        return out
    return jnp.concatenate(outputs, axis=0).reshape(batches, row_count, columns)


def solution(mesh):
    in_specs = (
        P(None, None, "tp"),
        P("tp", "pool"),
        P("tp", "pool"),
        P("pool", "tp"),
        P("pool", None, "tp"),
        P("pool", "tp", None),
        P(),
        P(),
    )
    return jax.shard_map(
        on_device, mesh=mesh, in_specs=in_specs, out_specs=P(None, None, "tp"), check_vma=False
    )
```

```python
import jax
import jax.numpy as jnp
from jax import lax
from jax.experimental import pallas as pl
from jax.experimental.pallas import tpu as pltpu
from jax.sharding import PartitionSpec as P

ADAPTER_SCALE = 2.0
VMEM_LIMIT = 48 * 1024 * 1024
BF16 = jnp.bfloat16
F32 = jnp.float32


def tile_of(size, choices):
    return next((c for c in choices if size % c == 0), size)


def exchange(x, axis, bit):
    return lax.ppermute(x, axis, [(i, i ^ bit) for i in range(lax.axis_size(axis))])


def params():
    return pltpu.CompilerParams(vmem_limit_bytes=VMEM_LIMIT)


def pick_pages(pool_index, page_table, row_adapter, expand_pages, page_count, pool_count):
    _, ranks, hidden = expand_pages.shape
    width = hidden // pool_count
    batches, row_count = row_adapter.shape

    def body(p_ref, table_ref, rows_ref, pages_ref, chosen_ref, mask_ref, *refs):
        outs, sems = refs[:batches], refs[batches]
        copies = []
        for m in range(batches):
            rows = rows_ref[m : m + 1, :]
            page = jnp.zeros_like(rows)
            for a in range(page_table.shape[0]):
                page = jnp.where(rows == a, table_ref[a], page)
            local = page - p_ref[0] * page_count
            owned = (local >= 0) & (local < page_count)
            mask_ref[m] = jnp.where(owned, 1.0, 0.0)
            chosen = jnp.max(jnp.where(owned, local, 0))
            chosen_ref[m] = chosen
            for q in range(pool_count):
                source = pages_ref.at[chosen, :, pl.ds(q * width, width)]
                copy = pltpu.make_async_copy(source, outs[m].at[q], sems.at[m * pool_count + q])
                copy.start()
                copies.append(copy)
        for copy in copies:
            copy.wait()

    smem = pl.BlockSpec(memory_space=pltpu.SMEM)
    vmem = pl.BlockSpec(memory_space=pltpu.VMEM)
    hbm = pl.BlockSpec(memory_space=pltpu.HBM)
    chosen, mask, *blocks = pl.pallas_call(
        body,
        in_specs=[smem, smem, vmem, hbm],
        out_specs=[smem, vmem] + [hbm] * batches,
        out_shape=[
            jax.ShapeDtypeStruct((batches,), jnp.int32),
            jax.ShapeDtypeStruct((batches, 1, row_count), F32),
        ]
        + [jax.ShapeDtypeStruct((pool_count, ranks, width), BF16)] * batches,
        scratch_shapes=[pltpu.SemaphoreType.DMA((batches * pool_count,))],
        compiler_params=params(),
        name="pick_pages",
    )(pool_index, page_table, row_adapter, expand_pages)
    return chosen, mask, blocks


def shrink(tp_index, chosen, mask, activations, shrink_pages, tp):
    batches, row_count, depth = activations.shape
    ranks = shrink_pages.shape[1]
    local = ranks // tp

    def body(t_ref, chosen_ref, page_ref, x_ref, mask_ref, keep_ref, send_ref):
        part = lax.dot_general(
            page_ref[...], x_ref[...], (((1,), (1,)), ((), ())), preferred_element_type=F32
        )
        part = jnp.where(mask_ref[...] > 0.5, part, 0.0)
        blocks = [part[k * local : (k + 1) * local] for k in range(tp)]
        for bit in range(tp.bit_length() - 1):
            flip = ((t_ref[0] >> bit) & 1) == 1
            blocks = [jnp.where(flip, blocks[k ^ (1 << bit)], blocks[k]) for k in range(tp)]
        for k in range(tp // 2):
            keep_ref[k] = blocks[2 * k]
            send_ref[k] = blocks[2 * k + 1]

    out_spec = pl.BlockSpec((tp // 2, local, row_count), lambda m, t, c: (0, 0, m))
    return pl.pallas_call(
        body,
        grid_spec=pltpu.PrefetchScalarGridSpec(
            num_scalar_prefetch=2,
            grid=(batches,),
            in_specs=[
                pl.BlockSpec((None, ranks, depth), lambda m, t, c: (c[m], 0, 0)),
                pl.BlockSpec((None, row_count, depth), lambda m, t, c: (m, 0, 0)),
                pl.BlockSpec((None, 1, row_count), lambda m, t, c: (m, 0, 0)),
            ],
            out_specs=[out_spec, out_spec],
        ),
        out_shape=[jax.ShapeDtypeStruct((tp // 2, local, batches * row_count), F32)] * 2,
        compiler_params=params(),
        name="shrink",
    )(tp_index, chosen, shrink_pages, activations, mask)


def project(tp_index, activations, group, start, rows, weight, wide=None, factors=None):
    tp = lax.axis_size("tp")
    block = rows // tp
    depth, hidden = weight.shape
    tile = tile_of(hidden, (896, 512, 256, 128))
    half = tp // 2
    order = [(m, r) for first in (0, 1) for m in group for r in range(first, tp, 2)]
    count = len(order)
    pieces = 0 if wide is None else len(factors)

    def body(t_ref, *refs):
        x_refs, refs = refs[:count], refs[count:]
        w_ref, refs = refs[0], refs[1:]
        if wide is not None:
            wide_refs, e_refs = refs[:count], refs[count : count + pieces]
            refs = refs[count + pieces :]
        keep_ref, send_ref, xs = refs[:3]

        @pl.when(pl.program_id(0) == 0)
        def _():
            for k, x_ref in enumerate(x_refs):
                xs[k * block : (k + 1) * block, :] = x_ref[...]
            if wide is not None:
                for k, r_ref in enumerate(wide_refs):
                    refs[3][k * block : (k + 1) * block, :] = r_ref[...]

        acc = jnp.dot(xs[...], w_ref[...], preferred_element_type=F32)
        if wide is not None:
            e_all = jnp.concatenate([e_ref[...] for e_ref in e_refs], axis=0)
            acc += jnp.dot(refs[3][...], e_all, preferred_element_type=F32)
        acc = acc.reshape(2, len(group), half, block, tile)
        keep_ref[...] = acc[0]
        send_ref[...] = acc[1].astype(BF16)

    first = start // block

    def x_spec(m, r, width):
        return pl.BlockSpec((None, block, width), lambda i, t: (m, first + (t[0] ^ r), 0))

    in_specs = [x_spec(m, r, depth) for m, r in order] + [pl.BlockSpec((depth, tile), lambda i, t: (0, i))]
    operands = [activations] * count + [weight]
    scratch = [pltpu.VMEM((count * block, depth), BF16)]
    if wide is not None:
        slots = wide.shape[-1]
        in_specs += [x_spec(m, r, slots) for m, r in order]
        in_specs += [pl.BlockSpec((slots // pieces, tile), lambda i, t: (0, i))] * pieces
        operands += [wide] * count + list(factors)
        scratch += [pltpu.VMEM((count * block, slots), BF16)]
    out_spec = pl.BlockSpec((len(group), half, block, tile), lambda i, t: (0, 0, 0, i))
    return pl.pallas_call(
        body,
        grid_spec=pltpu.PrefetchScalarGridSpec(
            num_scalar_prefetch=1,
            grid=(hidden // tile,),
            in_specs=in_specs,
            out_specs=[out_spec, out_spec],
            scratch_shapes=scratch,
        ),
        out_shape=[
            jax.ShapeDtypeStruct((len(group), half, block, hidden), F32),
            jax.ShapeDtypeStruct((len(group), half, block, hidden), BF16),
        ],
        compiler_params=params(),
        cost_estimate=pl.CostEstimate(
            flops=2 * count * block * depth * hidden, bytes_accessed=2 * depth * hidden, transcendentals=0
        ),
        name="gate" if wide is None else "up",
    )(tp_index, *operands)


def scatter_sum(keep, send, after=()):
    terms, bit = [keep], 1
    while True:
        last = terms[0].shape[1] == 1
        if last and after:
            send, *after = lax.optimization_barrier((send, *after))
        terms.append(exchange(send, "tp", bit))
        if last:
            terms = [x[:, 0] for x in terms]
            return (terms, after) if after else terms
        send = sum(x[:, 1::2].astype(F32) for x in terms).astype(send.dtype)
        terms = [x[:, 0::2] for x in terms]
        bit *= 2


def gather_rows(block):
    tp = lax.axis_size("tp")
    blocks = [block]
    bit = tp // 2
    found = {0: block}
    while bit:
        for r in list(found):
            found[r ^ bit] = exchange(found[r], "tp", bit)
        bit //= 2
    return [found[r] for r in range(tp)]


def down_project(pool_index, blocks, weight, first, columns):
    pool = lax.axis_size("pool")
    tp = len(blocks)
    block, depth = blocks[0].shape
    rows = tp * block
    half = pool // 2
    piece = rows // pool
    per_block = block // piece
    tile = tile_of(columns, (512, 256, 128))

    def body(p_ref, *refs):
        h_refs, w_ref, keep_ref, send_ref, hs = refs[:tp], *refs[tp:]

        @pl.when(pl.program_id(0) == 0)
        def _():
            for k in range(pool):
                q = p_ref[0] ^ k
                at = pl.multiple_of(((q & 1) * half + (q >> 1)) * piece, piece)
                j = k % per_block
                hs[pl.ds(at, piece), :] = h_refs[k // per_block][j * piece : (j + 1) * piece, :]

        acc = jnp.dot(hs[...], w_ref[...], preferred_element_type=F32)
        acc = acc.reshape(2, half, piece, tile)
        keep_ref[...] = acc[0]
        send_ref[...] = acc[1].astype(BF16)

    out_spec = pl.BlockSpec((half, piece, tile), lambda i, p: (0, 0, i))
    return pl.pallas_call(
        body,
        grid_spec=pltpu.PrefetchScalarGridSpec(
            num_scalar_prefetch=1,
            grid=(columns // tile,),
            in_specs=[pl.BlockSpec((block, depth), lambda i, p: (0, 0))] * tp
            + [pl.BlockSpec((depth, tile), lambda i, p: (0, first // tile + i))],
            out_specs=[out_spec, out_spec],
            scratch_shapes=[pltpu.VMEM((rows, depth), BF16)],
        ),
        out_shape=[
            jax.ShapeDtypeStruct((half, piece, columns), F32),
            jax.ShapeDtypeStruct((half, piece, columns), BF16),
        ],
        compiler_params=params(),
        cost_estimate=pl.CostEstimate(
            flops=2 * rows * depth * columns, bytes_accessed=2 * depth * columns, transcendentals=0
        ),
        name="down",
    )(pool_index, *blocks, weight)


def pool_sum(keep, send, after=()):
    terms, bit = [keep], 1
    while True:
        if bit == 2 and after:
            send, *after = lax.optimization_barrier((send, *after))
        terms.append(exchange(send, "pool", bit))
        if terms[0].shape[0] == 1:
            break
        send = sum(x[1::2].astype(F32) for x in terms).astype(BF16)
        terms = [x[0::2] for x in terms]
        bit *= 2
    parts = [(sum(x.astype(F32) for x in terms).astype(BF16), [0])]
    while bit:
        have = jnp.concatenate([x for x, _ in parts]) if len(parts) > 1 else parts[0][0]
        order = [q ^ bit for _, qs in parts for q in qs]
        parts.append((exchange(have, "pool", bit), order))
        bit //= 2
    return parts, after


def place(tp_index, pool_index, parts, out, shape, batch, start, first):
    pool = sum(len(qs) for _, qs in parts)
    tp = lax.axis_size("tp")
    _, piece, columns = parts[0][0].shape
    per_block = pool // tp

    def body(t_ref, p_ref, *refs):
        out_ref, sems = refs[-2:]
        copies = []
        for part_ref, (_, qs) in zip(refs, parts):
            for j, q in enumerate(qs):
                k = p_ref[0] ^ q
                block = t_ref[0] ^ (k // per_block)
                at = pl.multiple_of(start + (block * per_block + k % per_block) * piece, piece)
                target = out_ref.at[batch, pl.ds(at, piece), pl.ds(first, columns)]
                copies.append(pltpu.make_async_copy(part_ref.at[j], target, sems.at[q]))
        for copy in copies:
            copy.start()
        for copy in copies:
            copy.wait()

    held = [] if out is None else [out]
    return pl.pallas_call(
        body,
        in_specs=[pl.BlockSpec(memory_space=pltpu.SMEM)] * 2
        + [pl.BlockSpec(memory_space=pl.ANY)] * (len(parts) + len(held)),
        out_specs=pl.BlockSpec(memory_space=pl.ANY),
        out_shape=jax.ShapeDtypeStruct(shape, BF16),
        scratch_shapes=[pltpu.SemaphoreType.DMA((pool,))],
        input_output_aliases={2 + len(parts): 0} if held else {},
        compiler_params=params(),
        name="place",
    )(tp_index, pool_index, *[x for x, _ in parts], *held)


def by_index(x, index):
    for bit in range(x.shape[0].bit_length() - 1):
        pairs = x.reshape(-1, 2, 1 << bit, *x.shape[1:])
        x = jnp.where((index >> bit) & 1, pairs[:, ::-1], pairs).reshape(x.shape)
    return x


def on_device(
    activations,
    gate_matrix,
    up_weight,
    down_matrix,
    shrink_pages,
    expand_pages,
    row_adapter,
    page_table,
):
    pool = lax.axis_size("pool")
    tp = lax.axis_size("tp")
    pool_index = lax.axis_index("pool")
    tp_index = lax.axis_index("tp")
    p_scalar = pool_index.astype(jnp.int32).reshape(1)
    t_scalar = tp_index.astype(jnp.int32).reshape(1)
    batches, row_count, _ = activations.shape
    page_count = shrink_pages.shape[0]
    rank_local = expand_pages.shape[1]
    columns = down_matrix.shape[1]
    chunks = [(m, 0, row_count) for m in range(batches)]

    def across(x):
        return lax.all_to_all(x, "pool", split_axis=0, concat_axis=0, tiled=True)

    chosen, mask, picked = pick_pages(
        p_scalar, page_table, row_adapter, expand_pages, page_count, pool
    )
    factors = [across(picked[0])]
    low = shrink(t_scalar, chosen, mask, activations, shrink_pages, tp)
    low = sum(scatter_sum(*(x[None] for x in low)))
    low = ADAPTER_SCALE * low.astype(BF16)
    ready, rows_in = lax.optimization_barrier((low, activations))
    gate = project(t_scalar, rows_in, range(batches), 0, row_count, gate_matrix)
    wide, bit = ready, 1
    while 4 * bit < pool:
        wide = jnp.concatenate([wide, exchange(wide, "pool", bit)])
        bit *= 2
    gate, (wide, *outgoing) = scatter_sum(*gate, (wide, *picked[1:]))
    while bit < pool:
        wide = jnp.concatenate([wide, exchange(wide, "pool", bit)])
        bit *= 2
    wide = wide.reshape(pool, rank_local, -1)
    factors += [across(x) for x in outgoing]
    wide = by_index(wide, pool_index)
    wide = wide.reshape(pool * rank_local, batches * row_count).T
    wide = wide.reshape(batches, row_count, pool * rank_local)
    factors = [x.reshape(pool * rank_local, -1) for x in factors]
    apart = row_count % (16 * pool) == 0 and pool % tp == 0 and columns % 256 == 0
    out, outputs, waiting = None, [], None
    rows_in = activations
    for m, start, rows in chunks:
        up = project(t_scalar, rows_in, (m,), start, rows, up_weight, wide, [factors[m]])
        held = 0 if apart else len(gate) - 1
        up, gate[held:] = scatter_sum(*up, gate[held:])
        if waiting:
            width = columns // 2
            for first in range(0, columns, width):
                keep, send = down_project(p_scalar, waiting[1], down_matrix, first, width)
                if first:
                    send, up[-1] = lax.optimization_barrier((send, up[-1]))
                parts, _ = pool_sum(keep, send)
                out = place(
                    t_scalar, p_scalar, parts, out, (batches, row_count, columns), *waiting[0], first
                )
        gate_value = sum(x[m].astype(F32) for x in gate)
        up_value = sum(x[0].astype(F32) for x in up)
        hidden = (jax.nn.silu(gate_value) * up_value).astype(BF16)
        hidden, rows_in = lax.optimization_barrier((hidden, rows_in))
        blocks = gather_rows(hidden)
        if apart:
            waiting = ((m, start), blocks)
        else:
            here = by_index(jnp.stack(blocks), tp_index).reshape(rows, -1)
            partial = jnp.dot(here, down_matrix, preferred_element_type=F32)
            outputs.append(lax.psum(partial, "pool").astype(BF16))
    if not apart:
        return jnp.concatenate(outputs, axis=0).reshape(batches, row_count, columns)
    width = columns // 2
    for first in (0, width):
        parts, _ = pool_sum(*down_project(p_scalar, waiting[1], down_matrix, first, width))
        out = place(
            t_scalar, p_scalar, parts, out, (batches, row_count, columns), *waiting[0], first
        )
    return out


def solution(mesh):
    in_specs = (
        P(None, None, "tp"),
        P("tp", "pool"),
        P("tp", "pool"),
        P("pool", "tp"),
        P("pool", None, "tp"),
        P("pool", "tp", None),
        P(),
        P(),
    )
    return jax.shard_map(
        on_device, mesh=mesh, in_specs=in_specs, out_specs=P(None, None, "tp"), check_vma=False
    )
```
